512 devices in a mesh: row: 16 (over y, x_lo, core), loop: 32 (over x_hi, z).
Axes of the slice: x: 4 (x_hi: 2, x_lo: 2; x = x_hi * 2 + x_lo), y: 4, z: 16, core: 2. Of those that a mesh axis runs over, the one named last changes fastest.
Arguments:
- gradient: bfloat16 [8192, 28672], P('row', 'loop'), may hold values from -6 to 6
- left_basis: bfloat16 [8192, 512], P('row'), may hold values from -0.0625 to 0.0625
- right_basis: bfloat16 [28672, 8192], P('loop', 'row'), may hold values from -0.03125 to 0.03125
- first_moment: float32 [512, 8192], P('loop', 'row'), may hold values from -6 to 6
- second_moment: float32 [512, 8192], P('loop', 'row'), may hold values from 0.25 to 4
Outputs:
- update: bfloat16 [8192, 28672], P('row', 'loop')
- first_next: float32 [512, 8192], P('loop', 'row')
- second_next: float32 [512, 8192], P('loop', 'row')
The draws below stay inside these ranges and needn't reach their ends.
All inputs are finite; a program needn't handle non-finite values.
Results may differ from the reference program's by a relative error of at most 0.0075.
Values may be sent and summed in bfloat16 or wider, within the bound.
A program may use at most 64 MiB of HBM per device.

```python
import math
import jax
import jax.numpy as jnp

D = 8192
N = 28672
R = 512
C = 8192


def shard_levels(key, extent, shards, smallest, largest):
    factor_of, own = 1.0, jax.random.fold_in(key, 6)
    for position, parts in shards:
        draws = jnp.exp(jax.random.uniform(jax.random.fold_in(own, position), (parts,), jnp.float32, smallest / len(shards), largest / len(shards)))
        factor_of = factor_of * jnp.repeat(draws, extent[position] // parts).reshape([-1 if axis == position else 1 for axis in range(len(extent))])
    return factor_of


def gaussian(key, dims, scale, most, pieces=(), held_as=jnp.bfloat16):
    gain = shard_levels(key, dims, pieces, -0.22, 0.18) if pieces else 1.0
    values = jax.random.normal(key, dims, jnp.float32) * scale * gain
    return jnp.minimum(jnp.maximum(values, -most), most).astype(held_as)


def setup_inputs(seed: int = 0) -> dict:
    seeds = jax.random.split(jax.random.key(seed), 6)
    gradient = gaussian(seeds[0], (D, N), 1.0, 6.0, ((0, 16), (1, 32)))
    left_basis = gaussian(seeds[1], (D, R), D ** -0.5, 0.0625, ((0, 16),))
    right_basis = gaussian(seeds[2], (N, C), N ** -0.5, 0.03125, ((0, 32), (1, 16)))
    first_moment = gaussian(seeds[3], (R, C), 1.0, 6.0, ((0, 32), (1, 16)), jnp.float32)
    second_moment = jnp.clip(jnp.exp(math.log(4.0) - 2.7725887 * jax.random.uniform(seeds[4], (R, C), jnp.float32) ** shard_levels(seeds[4], (R, C), ((0, 32), (1, 16)), -0.2, 0.2)), 0.25, 4.0)
    return {"gradient": gradient, "left_basis": left_basis, "right_basis": right_basis, "first_moment": first_moment, "second_moment": second_moment}


def reference(gradient, left_basis, right_basis, first_moment, second_moment):
    rotated = jnp.dot(left_basis.T, gradient, preferred_element_type=jnp.float32)
    rotated_half = rotated.astype(jnp.bfloat16)
    projected = jnp.dot(rotated_half, right_basis, preferred_element_type=jnp.float32)
    first_next = 0.9 * first_moment + 0.1 * projected
    second_next = 0.95 * second_moment + 0.05 * projected * projected
    direction = (first_next / (jnp.sqrt(second_next) + 1e-08)).astype(jnp.bfloat16)
    back = jnp.dot(direction, right_basis.T, preferred_element_type=jnp.float32).astype(jnp.bfloat16)
    update = jnp.dot(left_basis, back, preferred_element_type=jnp.float32).astype(jnp.bfloat16)
    return (update, first_next, second_next)
```

```python
import functools

import jax
import jax.numpy as jnp
from jax import lax
from jax.experimental import pallas as pl
from jax.experimental.pallas import tpu as pltpu
from jax.sharding import PartitionSpec as P

MESH = pl.DeviceIdType.MESH
BF16 = jnp.bfloat16
F32 = jnp.float32
RING = 16
QUAD = 4


def dot(a, b):
    return jnp.dot(a, b, preferred_element_type=F32)


def kernel(
    g_hbm, l_hbm, q_hbm, m1_ref, m2_ref,
    update_ref, first_ref, second_ref,
    g, lb, q, lt, qt,
    xs, xr, hs, rr, keep, full,
    ps, own, bq, bs, br, dirp, dirf,
    in_sem, core_s, core_r, sum_s, sum_r, all_s, all_r, relay_s, relay_r,
    near_s, near_r, far_s, far_r, dfar_s, dfar_r, dnear_s, dnear_r,
):
    row, loop = lax.axis_index("row"), lax.axis_index("loop")
    core, x, y = row % 2, (row // 2) % 2, row // 4
    xh, z = loop // RING, loop % RING
    chip = y * 2 + x
    sign = 1 - 2 * core

    loads = [
        pltpu.make_async_copy(src, dst, in_sem.at[n])
        for n, (src, dst) in enumerate(((l_hbm, lb), (g_hbm, g), (q_hbm, q)))
    ]
    for load in loads:
        load.start()

    sibling = (row + 1 - 2 * core, loop)

    def chip_of(m):
        py = y
        if m & 2:
            py = py + 1 - 2 * (py % 2)
        if m & 4:
            py = (py + 2) % 4
        px = 1 - x if m & 1 else x
        return py * 2 + px

    def in_row(m):
        return (chip_of(m) * 2 + core, loop)

    def in_loop(plane, offset):
        return (row, plane * RING + (z + offset + RING) % RING)

    offsets = (2 * sign, 1, -1)
    here, there = xh, 1 - xh

    barrier = pltpu.get_barrier_semaphore()
    senders = [sibling] + [in_row(m) for m in range(1, 8)]
    senders += [in_loop(plane, -o) for plane in (here, there) for o in offsets]
    senders += [in_loop(there, 0)] + [in_loop(here, QUAD * t) for t in (1, 2, 3)]
    for device in senders:
        pl.semaphore_signal(barrier, inc=1, device_id=device, device_id_type=MESH)

    loads[0].wait()
    turned = lb[...].T
    for plane in range(2):
        for a in range(QUAD):
            for s in range(QUAD):
                src, dst = plane * RING + a * QUAD + s, plane * RING + s * QUAD + a
                lt[dst * 16 : dst * 16 + 16, :] = turned[src * 16 : src * 16 + 16, :]
    loads[1].wait()

    def send(src, dst, s_sem, r_sem, device):
        copy = pltpu.make_async_remote_copy(
            src_ref=src, dst_ref=dst, send_sem=s_sem, recv_sem=r_sem,
            device_id=device, device_id_type=MESH,
        )
        copy.start()
        return copy

    sent = []

    def row_sum(turn, part, after_own, after_other):
        block = [128 * (1 - y // 2), 128 * (y // 2)]
        crossing = []
        for c in range(2):
            xs[turn, c] = part(256 * (1 - core) + block[c]).astype(BF16)
            if turn == 0 and c == 0:
                pl.semaphore_wait(barrier, 18)
            crossing.append(
                send(xs.at[turn, c], xr.at[turn, c], core_s.at[turn, c], core_r.at[turn, c], sibling)
            )
        summing = {}
        for c, relations in ((0, (5, 7, 4, 6)), (1, (3, 2, 1))):
            mine = part(256 * core + block[c])
            crossing[c].wait_recv()
            both = mine + xr[turn, c].astype(F32)
            hs[turn, c] = both.astype(BF16)
            if c == 1:
                keep[...] = both
            for m in relations:
                piece = hs.at[turn, c, pl.ds(pl.multiple_of(32 * (chip_of(m) % 4), 32), 32)]
                summing[m] = send(
                    piece, rr.at[turn, m - 1], sum_s.at[turn, m - 1], sum_r.at[turn, m - 1], in_row(m)
                )
        total = keep[pl.ds(pl.multiple_of(32 * (chip % 4), 32), 32), :]
        for m in (1, 2, 6, 4, 3, 7, 5):
            summing[m].wait_recv()
            total = total + rr[turn, m - 1].astype(F32)

        def rows(half, m):
            return pl.ds(pl.multiple_of(256 * half + 32 * chip_of(m), 32), 32)

        full[turn, rows(core, 0), :] = total.astype(BF16)
        spreading = {}
        for m in (5, 7, 3, 4, 6, 2, 1):
            piece = full.at[turn, rows(core, 0)]
            spreading[m] = send(
                piece, piece, all_s.at[turn, m - 1], all_r.at[turn, m - 1], in_row(m)
            )
        relays = []
        for m in (0, 1, 2, 6, 4, 3, 7, 5):
            piece = full.at[turn, rows(core, m)]
            if m:
                landed = pltpu.make_async_remote_copy(
                    src_ref=piece, dst_ref=piece, send_sem=all_s.at[turn, m - 1],
                    recv_sem=all_r.at[turn, m - 1], device_id=in_row(m), device_id_type=MESH,
                )
                landed.wait_recv()
            relays.append(
                send(piece, piece, relay_s.at[turn, m], relay_r.at[turn, m], sibling)
            )
        after_own()
        for m in range(8):
            piece = full.at[turn, rows(1 - core, m)]
            landed = pltpu.make_async_remote_copy(
                src_ref=piece, dst_ref=piece, send_sem=relay_s.at[turn, m],
                recv_sem=relay_r.at[turn, m], device_id=sibling, device_id_type=MESH,
            )
            landed.wait_recv()
        after_other()
        sent.extend(crossing)
        sent.extend(summing.values())
        sent.extend(spreading.values())
        sent.extend(relays)

    def project(half):
        first_row = pl.multiple_of(256 * half, 256)
        value = dot(full[0, pl.ds(first_row, 256), :], q[...])
        own[half] = value
        ps[pl.ds(first_row, 256), :] = value.astype(BF16)
        relation = (half + xh) % 2
        for t in (2, 1, 3, 0):
            for d, o in enumerate(offsets):
                zt = (z + o + RING) % RING
                at = half * RING + (zt % QUAD) * QUAD + (zt // QUAD + t) % QUAD
                slot = relation * 3 + d
                sent.append(
                    send(
                        ps.at[pl.ds(pl.multiple_of(16 * at, 16), 16)], bq.at[slot, t],
                        near_s.at[slot, t], near_r.at[slot, t], in_loop(half, o),
                    )
                )

    def project_own():
        loads[2].wait()
        project(core)

    def project_other():
        project(1 - core)
        for t in (2, 1, 3, 0):
            at = there * RING + (z % QUAD) * QUAD + (z // QUAD + t) % QUAD
            sent.append(
                send(
                    ps.at[pl.ds(pl.multiple_of(16 * at, 16), 16)], bq.at[6, t],
                    near_s.at[6, t], near_r.at[6, t], in_loop(there, 0),
                )
            )

    row_sum(
        0,
        lambda r: dot(lt[pl.ds(pl.multiple_of(r, 128), 128), :], g[...]),
        project_own,
        project_other,
    )
    qt[...] = q[...].T

    def landing(dst, s_sem, r_sem, device):
        pltpu.make_async_remote_copy(
            src_ref=dst, dst_ref=dst, send_sem=s_sem, recv_sem=r_sem,
            device_id=device, device_id_type=MESH,
        ).wait_recv()

    far = {}
    for t in (2, 1, 3, 0):
        at = (z % QUAD) * QUAD + (z // QUAD + t) % QUAD
        total = own[here, pl.ds(pl.multiple_of(16 * at, 16), 16), :]
        for slot in range(7):
            landing(bq.at[slot, t], near_s.at[slot, t], near_r.at[slot, t], sibling)
            total = total + bq[slot, t].astype(F32)
        if t:
            bs[t - 1] = total.astype(BF16)
            far[t] = send(
                bs.at[t - 1], br.at[t - 1], far_s.at[t - 1], far_r.at[t - 1], in_loop(here, QUAD * t)
            )
    for t in (1, 3, 2):
        far[t].wait_recv()
        total = total + br[t - 1].astype(F32)
    sent.extend(far.values())

    first = 0.9 * m1_ref[...] + 0.1 * total
    second = 0.95 * m2_ref[...] + 0.05 * total * total
    first_ref[...] = first
    second_ref[...] = second

    def slice_of(plane, zz):
        return pl.ds(pl.multiple_of(16 * (plane * RING + (zz % QUAD) * QUAD + zz // QUAD), 16), 16)

    def moved(o):
        return (z + o + RING) % RING

    dirp[slice_of(here, z), :] = (first / (jnp.sqrt(second) + 1e-08)).astype(BF16)

    mine = dirp.at[slice_of(here, z)]
    for t in (2, 1, 3):
        sent.append(send(mine, mine, dfar_s.at[t - 1], dfar_r.at[t - 1], in_loop(here, QUAD * t)))
    partners = [(here, o) for o in offsets] + [(there, o) for o in offsets] + [(there, 0)]
    for t in (0, 1, 3, 2):
        piece = dirp.at[slice_of(here, moved(-QUAD * t))]
        if t:
            landing(piece, dfar_s.at[t - 1], dfar_r.at[t - 1], sibling)
        for n, (plane, o) in enumerate(partners):
            sent.append(send(piece, piece, dnear_s.at[n, t], dnear_r.at[n, t], in_loop(plane, o)))
    for t in (0, 1, 3, 2):
        for n, (plane, o) in enumerate(partners):
            piece = dirp.at[slice_of(plane, moved(-o - QUAD * t))]
            landing(piece, dnear_s.at[n, t], dnear_r.at[n, t], sibling)

    for plane in range(2):
        for a in range(QUAD):
            for s in range(QUAD):
                dst, src = plane * RING + a * QUAD + s, plane * RING + s * QUAD + a
                dirf[dst * 16 : dst * 16 + 16, :] = dirp[src * 16 : src * 16 + 16, :]

    def nothing():
        pass

    row_sum(
        1,
        lambda r: dot(dirf[pl.ds(pl.multiple_of(r, 128), 128), :], qt[...]),
        nothing,
        nothing,
    )
    for c in range(4):
        update_ref[c * 128 : c * 128 + 128, :] = dot(lb[c * 128 : c * 128 + 128, :], full[1]).astype(BF16)
    for copy in sent:
        copy.wait_send()


def per_device(gradient, left_basis, right_basis, first_moment, second_moment):
    depth, width = gradient.shape
    window = left_basis.shape[1]
    cols = right_basis.shape[1]
    mine = first_moment.shape[0]
    sems = pltpu.SemaphoreType.DMA
    return pl.pallas_call(
        kernel,
        out_shape=(
            jax.ShapeDtypeStruct((depth, width), BF16),
            jax.ShapeDtypeStruct(first_moment.shape, F32),
            jax.ShapeDtypeStruct(second_moment.shape, F32),
        ),
        in_specs=[pl.BlockSpec(memory_space=pl.ANY)] * 3 + [pl.BlockSpec(memory_space=pltpu.VMEM)] * 2,
        out_specs=[pl.BlockSpec(memory_space=pltpu.VMEM)] * 3,
        scratch_shapes=[
            pltpu.VMEM((depth, width), BF16),
            pltpu.VMEM((depth, window), BF16),
            pltpu.VMEM((width, cols), BF16),
            pltpu.VMEM((window, depth), BF16),
            pltpu.VMEM((cols, width), BF16),
            pltpu.VMEM((2, 2, 128, width), BF16),
            pltpu.VMEM((2, 2, 128, width), BF16),
            pltpu.VMEM((2, 2, 128, width), BF16),
            pltpu.VMEM((2, 7, 32, width), BF16),
            pltpu.VMEM((128, width), F32),
            pltpu.VMEM((2, window, width), BF16),
            pltpu.VMEM((window, cols), BF16),
            pltpu.VMEM((2, window // 2, cols), F32),
            pltpu.VMEM((7, 4, mine, cols), BF16),
            pltpu.VMEM((3, mine, cols), BF16),
            pltpu.VMEM((3, mine, cols), BF16),
            pltpu.VMEM((window, cols), BF16),
            pltpu.VMEM((window, cols), BF16),
            sems((3,)),
            sems((2, 2)), sems((2, 2)),
            sems((2, 7)), sems((2, 7)),
            sems((2, 7)), sems((2, 7)),
            sems((2, 8)), sems((2, 8)),
            sems((7, 4)), sems((7, 4)),
            sems((3,)), sems((3,)),
            sems((3,)), sems((3,)),
            sems((7, 4)), sems((7, 4)),
        ],
        compiler_params=pltpu.CompilerParams(
            collective_id=0, has_side_effects=True, vmem_limit_bytes=40 << 20
        ),
        name="soap",
    )(gradient, left_basis, right_basis, first_moment, second_moment)


def solution(mesh):
    placed = (
        P("row", "loop"),
        P("row", None),
        P("loop", "row"),
        P("loop", "row"),
        P("loop", "row"),
    )
    return jax.shard_map(
        per_device,
        mesh=mesh,
        in_specs=placed,
        out_specs=(P("row", "loop"), P("loop", "row"), P("loop", "row")),
        check_vma=False,
    )
```

```python
import functools

import jax
import jax.numpy as jnp
from jax import lax
from jax.experimental import pallas as pl
from jax.experimental.pallas import tpu as pltpu
from jax.sharding import PartitionSpec as P

MESH = pl.DeviceIdType.MESH
BF16 = jnp.bfloat16
F32 = jnp.float32
RING = 16
QUAD = 4


def dot(a, b):
    return jnp.dot(a, b, preferred_element_type=F32)


def kernel(
    g_hbm, l_hbm, q_hbm, m1_hbm, m2_hbm,
    back_hbm, left_hbm, projected_ref,
    g, lb, q, m1, m2, lt, lp, qt,
    xs, xr, hs, rr, keep, full,
    own, ps, bq, near, bs, br, dirp, dirf,
    in_sem, out_sem, core_s, core_r, sum_s, sum_r, all_s, all_r, relay_s, relay_r,
    near_s, near_r, far_s, far_r, dfar_s, dfar_r, dnear_s, dnear_r,
):
    row, loop = lax.axis_index("row"), lax.axis_index("loop")
    core, x, y = row % 2, (row // 2) % 2, row // 4
    here, z = loop // RING, loop % RING
    there = 1 - here
    chip = y * 2 + x
    offsets = (2 - 4 * core, 1, -1)
    partners = [(there, o) for o in offsets] + [(there, 0)] + [(here, o) for o in offsets]
    sibling = (row + 1 - 2 * core, loop)

    loads = [
        pltpu.make_async_copy(src, dst, in_sem.at[n])
        for n, (src, dst) in enumerate(
            ((l_hbm, lb), (g_hbm, g), (q_hbm, q), (m1_hbm, m1), (m2_hbm, m2))
        )
    ]
    for load in loads:
        load.start()

    def chip_of(m):
        py = y
        if m & 2:
            py = py + 1 - 2 * (py % 2)
        if m & 4:
            py = (py + 2) % 4
        px = 1 - x if m & 1 else x
        return py * 2 + px

    def in_row(m):
        return (chip_of(m) * 2 + core, loop)

    def moved(o):
        return (z + o + RING) % RING

    def at(plane, o):
        return (row, plane * RING + moved(o))

    barrier = pltpu.get_barrier_semaphore()
    senders = [at(here, QUAD * t) for t in (2, 1, 3)] + [at(plane, -o) for plane, o in partners]
    senders += [in_row(m) for m in range(1, 8)] + [sibling]
    for device in senders:
        pl.semaphore_signal(barrier, inc=1, device_id=device, device_id_type=MESH)

    loads[0].wait()
    lb[...] = lb[...].T
    for plane in range(2):
        for s in range(QUAD):
            for a in range(0, QUAD, 2):
                two = [
                    lb[16 * (plane * RING + i * QUAD + s) : 16 * (plane * RING + i * QUAD + s + 1), :].astype(F32)
                    for i in (a, a + 1)
                ]
                for c in range(2):
                    dst = 256 * c + 128 * plane + 32 * s + 8 * a
                    lt[dst : dst + 16, :] = jnp.concatenate(
                        [v[8 * c : 8 * c + 8] for v in two], axis=0
                    ).astype(BF16)
    loads[1].wait()

    sent = []

    def send(src, dst, s_sem, r_sem, device):
        copy = pltpu.make_async_remote_copy(
            src_ref=src, dst_ref=dst, send_sem=s_sem, recv_sem=r_sem,
            device_id=device, device_id_type=MESH,
        )
        copy.start()
        sent.append(copy)

    def landing(dst, s_sem, r_sem):
        pltpu.make_async_remote_copy(
            src_ref=dst, dst_ref=dst, send_sem=s_sem, recv_sem=r_sem,
            device_id=sibling, device_id_type=MESH,
        ).wait_recv()

    def rows(start, count):
        return pl.ds(pl.multiple_of(start, count), count)

    def packed(value):
        n, w = value.shape[0] // 8, value.shape[1] // 2
        value = value.reshape(n, 8, 2 * w)
        return jnp.concatenate([value[:, :, :w], value[:, :, w:]], axis=1).reshape(16 * n, w)

    def unpacked(value):
        n, w = value.shape[0] // 16, value.shape[1]
        value = value.reshape(n, 16, w)
        return jnp.concatenate([value[:, :8], value[:, 8:]], axis=2).reshape(8 * n, 2 * w)

    def row_sum(turn, c, part):
        i = 2 * turn + c
        xs[i] = part(128 * (1 - core)).astype(BF16)
        if i == 0:
            pl.semaphore_wait(barrier, len(senders))
        send(xs.at[i], xr.at[i], core_s.at[i], core_r.at[i], sibling)
        yield
        mine = part(128 * core)
        landing(xr.at[i], core_s.at[i], core_r.at[i])
        both = mine + xr[i].astype(F32)
        hs[i] = both.astype(BF16)
        keep[i] = both
        for m in (5, 4, 7, 3, 6, 2, 1):
            send(
                hs.at[i, rows(16 * chip_of(m), 16)], rr.at[i, m - 1],
                sum_s.at[i, m - 1], sum_r.at[i, m - 1], in_row(m),
            )
        yield
        total = keep[i, rows(16 * chip, 16), :]
        for m in (1, 2, 6, 3, 7, 4, 5):
            landing(rr.at[i, m - 1], sum_s.at[i, m - 1], sum_r.at[i, m - 1])
            total = total + rr[i, m - 1].astype(F32)

        def piece(half, m):
            return full.at[turn, rows(256 * c + 128 * half + 16 * chip_of(m), 16)]

        own_piece = piece(core, 0)
        own_piece[...] = total.astype(BF16)
        for m in (5, 4, 7, 3, 6, 2, 1):
            send(own_piece, own_piece, all_s.at[i, m - 1], all_r.at[i, m - 1], in_row(m))
        send(own_piece, own_piece, relay_s.at[i, 0], relay_r.at[i, 0], sibling)
        yield
        for m in (1, 2, 6, 3, 7, 4, 5):
            landing(piece(core, m), all_s.at[i, m - 1], all_r.at[i, m - 1])
            send(piece(core, m), piece(core, m), relay_s.at[i, m], relay_r.at[i, m], sibling)
        for m in range(8):
            landing(piece(1 - core, m), relay_s.at[i, m], relay_r.at[i, m])

    def chunk(c):
        yield from row_sum(
            0, c, lambda r: dot(lt[pl.ds(pl.multiple_of(256 * c + r, 128), 128), :], g[...])
        )

        value = packed(dot(full[0, 256 * c : 256 * c + 256, :], q[...]))
        own[c] = value
        ps[c] = value.astype(BF16)
        for n, (plane, o) in enumerate(partners):
            send(
                ps.at[c, rows(64 * (plane * QUAD + moved(o) % QUAD), 64)], bq.at[c, n],
                near_s.at[c, n], near_r.at[c, n], at(plane, o),
            )
        yield
        total = own[c, rows(64 * (here * QUAD + z % QUAD), 64), :]
        for n in (4, 5, 6, 3, 1, 2, 0):
            landing(bq.at[c, n], near_s.at[c, n], near_r.at[c, n])
            total = total + bq[c, n].astype(F32)
        near[c] = total
        bs[c] = total.astype(BF16)
        for t in (2, 1, 3):
            send(
                bs.at[c, rows(16 * ((z // QUAD + t) % QUAD), 16)], br.at[c, t - 1],
                far_s.at[c, t - 1], far_r.at[c, t - 1], at(here, QUAD * t),
            )
        yield
        total = near[c, rows(16 * (z // QUAD), 16), :]
        for t in (1, 3, 2):
            landing(br.at[c, t - 1], far_s.at[c, t - 1], far_r.at[c, t - 1])
            total = total + br[c, t - 1].astype(F32)
        total = unpacked(total)
        mine = slice(8 * c, 8 * c + 8)
        projected_ref[mine, :] = total
        first = 0.9 * m1[mine, :] + 0.1 * total
        second = 0.95 * m2[mine, :] + 0.05 * total * total

        def slice_of(plane, o):
            zz = moved(o)
            return dirp.at[c, rows(16 * (plane * RING + (zz % QUAD) * QUAD + zz // QUAD), 16)]

        piece = slice_of(here, 0)
        piece[...] = packed(first / (jnp.sqrt(second) + 1e-08)).astype(BF16)
        for t in (2, 1, 3):
            send(piece, piece, dfar_s.at[c, t - 1], dfar_r.at[c, t - 1], at(here, QUAD * t))

        def forward(t):
            piece = slice_of(here, -QUAD * t)
            for n, (plane, o) in enumerate(partners):
                send(piece, piece, dnear_s.at[c, n, t], dnear_r.at[c, n, t], at(plane, o))

        forward(0)
        yield
        for t in (1, 3, 2):
            landing(slice_of(here, -QUAD * t), dfar_s.at[c, t - 1], dfar_r.at[c, t - 1])
            forward(t)
        yield
        for t in (0, 1, 3, 2):
            for n, (plane, o) in enumerate(partners):
                landing(slice_of(plane, -o - QUAD * t), dnear_s.at[c, n, t], dnear_r.at[c, n, t])
        dirf[c] = unpacked(dirp[c].astype(F32)).astype(BF16)
        yield from row_sum(1, c, lambda r: dot(dirf[c, rows(r, 128), :], qt[...]))
        done = pltpu.make_async_copy(
            full.at[1, pl.ds(256 * c, 256)], back_hbm.at[pl.ds(256 * c, 256)], out_sem.at[c]
        )
        done.start()
        finals.append(done)

    finals = []
    chunks = [chunk(0), chunk(1)]
    step = 0
    while chunks:
        for each in list(chunks):
            if next(each, finals) is finals:
                chunks.remove(each)
        step += 1
        if step == 2:
            loads[2].wait()
            qt[...] = q[...].T
        if step == 3:
            lp[...] = lt[...].T
            left = pltpu.make_async_copy(lp, left_hbm, out_sem.at[2])
            left.start()
            finals.append(left)
            loads[3].wait()
            loads[4].wait()
    for copy in sent:
        copy.wait_send()
    for copy in finals:
        copy.wait()


def finish(left_ref, back_ref, projected_ref, m1_ref, m2_ref, update_ref, first_ref, second_ref):
    projected = projected_ref[...]
    first_ref[...] = 0.9 * m1_ref[...] + 0.1 * projected
    second_ref[...] = 0.95 * m2_ref[...] + 0.05 * projected * projected
    update_ref[...] = dot(left_ref[...], back_ref[...]).astype(BF16)


def per_device(gradient, left_basis, right_basis, first_moment, second_moment):
    depth, width = gradient.shape
    window = left_basis.shape[1]
    cols = right_basis.shape[1]
    mine = first_moment.shape[0]
    sems = pltpu.SemaphoreType.DMA
    back, left, projected = pl.pallas_call(
        kernel,
        out_shape=(
            jax.ShapeDtypeStruct((window, width), BF16),
            jax.ShapeDtypeStruct((depth, window), BF16),
            jax.ShapeDtypeStruct((mine, cols), F32),
        ),
        in_specs=[pl.BlockSpec(memory_space=pl.ANY)] * 5,
        out_specs=[pl.BlockSpec(memory_space=pl.ANY)] * 2 + [pl.BlockSpec(memory_space=pltpu.VMEM)],
        scratch_shapes=[
            pltpu.VMEM((depth, width), BF16),
            pltpu.VMEM((depth, window), BF16),
            pltpu.VMEM((width, cols), BF16),
            pltpu.VMEM((mine, cols), F32),
            pltpu.VMEM((mine, cols), F32),
            pltpu.VMEM((window, depth), BF16),
            pltpu.VMEM((depth, window), BF16),
            pltpu.VMEM((cols, width), BF16),
            pltpu.VMEM((4, 128, width), BF16),
            pltpu.VMEM((4, 128, width), BF16),
            pltpu.VMEM((4, 128, width), BF16),
            pltpu.VMEM((4, 7, 16, width), BF16),
            pltpu.VMEM((4, 128, width), F32),
            pltpu.VMEM((2, window, width), BF16),
            pltpu.VMEM((2, window, cols // 2), F32),
            pltpu.VMEM((2, window, cols // 2), BF16),
            pltpu.VMEM((2, 7, 64, cols // 2), BF16),
            pltpu.VMEM((2, 64, cols // 2), F32),
            pltpu.VMEM((2, 64, cols // 2), BF16),
            pltpu.VMEM((2, 3, mine, cols // 2), BF16),
            pltpu.VMEM((2, window, cols // 2), BF16),
            pltpu.VMEM((2, window // 2, cols), BF16),
            sems((5,)), sems((3,)),
            sems((4,)), sems((4,)),
            sems((4, 7)), sems((4, 7)),
            sems((4, 7)), sems((4, 7)),
            sems((4, 8)), sems((4, 8)),
            sems((2, 7)), sems((2, 7)),
            sems((2, 3)), sems((2, 3)),
            sems((2, 3)), sems((2, 3)),
            sems((2, 7, 4)), sems((2, 7, 4)),
        ],
        compiler_params=pltpu.CompilerParams(
            collective_id=0, has_side_effects=True, vmem_limit_bytes=60 << 20
        ),
        name="soap",
    )(gradient, left_basis, right_basis, first_moment, second_moment)
    block = 128
    small = pl.BlockSpec((mine, cols), lambda i: (0, 0))
    return pl.pallas_call(
        finish,
        grid=(depth // block,),
        out_shape=(
            jax.ShapeDtypeStruct((depth, width), BF16),
            jax.ShapeDtypeStruct(first_moment.shape, F32),
            jax.ShapeDtypeStruct(second_moment.shape, F32),
        ),
        in_specs=[
            pl.BlockSpec((block, window), lambda i: (i, 0)),
            pl.BlockSpec((window, width), lambda i: (0, 0)),
            small, small, small,
        ],
        out_specs=[pl.BlockSpec((block, width), lambda i: (i, 0)), small, small],
        compiler_params=pltpu.CompilerParams(vmem_limit_bytes=60 << 20),
        name="finish",
    )(left, back, projected, first_moment, second_moment)


def solution(mesh):
    placed = (
        P("row", "loop"),
        P("row", None),
        P("loop", "row"),
        P("loop", "row"),
        P("loop", "row"),
    )
    return jax.shard_map(
        per_device,
        mesh=mesh,
        in_specs=placed,
        out_specs=(P("row", "loop"), P("loop", "row"), P("loop", "row")),
        check_vma=False,
    )
```

```python
import functools

import jax
import jax.numpy as jnp
from jax import lax
from jax.experimental import pallas as pl
from jax.experimental.pallas import tpu as pltpu
from jax.sharding import PartitionSpec as P

MESH = pl.DeviceIdType.MESH
BF16 = jnp.bfloat16
F32 = jnp.float32
RING = 16
QUAD = 4


def dot(a, b):
    return jnp.dot(a, b, preferred_element_type=F32)


def kernel(
    g_hbm, l_hbm, q_hbm, m1_hbm, m2_hbm,
    back_hbm, left_hbm, projected_ref,
    g, lb, q, m1, m2, lt, lp, qt,
    xs, xr, hs, rr, keep, full,
    own, ps, bq, near, bs, br, dirp, dirf,
    in_sem, out_sem, core_s, core_r, sum_s, sum_r, all_s, all_r, relay_s, relay_r,
    near_s, near_r, far_s, far_r, dfar_s, dfar_r, dnear_s, dnear_r, met,
):
    row, loop = lax.axis_index("row"), lax.axis_index("loop")
    core, x, y = row % 2, (row // 2) % 2, row // 4
    here, z = loop // RING, loop % RING
    there = 1 - here
    chip = y * 2 + x
    offsets = (2 - 4 * core, 1, -1)
    partners = [(there, o) for o in offsets] + [(there, 0)] + [(here, o) for o in offsets]
    sibling = (row + 1 - 2 * core, loop)

    loads = [
        pltpu.make_async_copy(src, dst, in_sem.at[n])
        for n, (src, dst) in enumerate(
            ((l_hbm, lb), (g_hbm, g), (q_hbm, q), (m1_hbm, m1), (m2_hbm, m2))
        )
    ]
    for load in loads:
        load.start()

    def chip_of(m):
        py = y
        if m & 2:
            py = py + 1 - 2 * (py % 2)
        if m & 4:
            py = (py + 2) % 4
        px = 1 - x if m & 1 else x
        return py * 2 + px

    def in_row(m):
        return (chip_of(m) * 2 + core, loop)

    def moved(o):
        return (z + o + RING) % RING

    def at(plane, o):
        return (row, plane * RING + moved(o))

    barrier = pltpu.get_barrier_semaphore()
    greeted = [at(here, 1), at(here, -1), at(there, 0)] + [in_row(m) for m in range(1, 8)] + [sibling]

    def greet(sem, devices):
        for device in devices:
            pl.semaphore_signal(sem, inc=1, device_id=device, device_id_type=MESH)

    greet(barrier, greeted)

    loads[0].wait()
    lb[...] = lb[...].T
    for plane in range(2):
        for s in range(QUAD):
            for a in range(0, QUAD, 2):
                two = [
                    lb[16 * (plane * RING + i * QUAD + s) : 16 * (plane * RING + i * QUAD + s + 1), :].astype(F32)
                    for i in (a, a + 1)
                ]
                for c in range(2):
                    dst = 256 * c + 128 * plane + 32 * s + 8 * a
                    lt[dst : dst + 16, :] = jnp.concatenate(
                        [v[8 * c : 8 * c + 8] for v in two], axis=0
                    ).astype(BF16)
    loads[1].wait()

    sent = []

    def send(src, dst, s_sem, r_sem, device):
        copy = pltpu.make_async_remote_copy(
            src_ref=src, dst_ref=dst, send_sem=s_sem, recv_sem=r_sem,
            device_id=device, device_id_type=MESH,
        )
        copy.start()
        sent.append(copy)

    def landing(dst, s_sem, r_sem):
        pltpu.make_async_remote_copy(
            src_ref=dst, dst_ref=dst, send_sem=s_sem, recv_sem=r_sem,
            device_id=sibling, device_id_type=MESH,
        ).wait_recv()

    def rows(start, count):
        return pl.ds(pl.multiple_of(start, count), count)

    def packed(value):
        n, w = value.shape[0] // 8, value.shape[1] // 2
        value = value.reshape(n, 8, 2 * w)
        return jnp.concatenate([value[:, :, :w], value[:, :, w:]], axis=1).reshape(16 * n, w)

    def unpacked(value):
        n, w = value.shape[0] // 16, value.shape[1]
        value = value.reshape(n, 16, w)
        return jnp.concatenate([value[:, :8], value[:, 8:]], axis=2).reshape(8 * n, 2 * w)

    def row_sum(turn, c, part):
        i = 2 * turn + c
        xs[i] = part(128 * (1 - core)).astype(BF16)
        if i == 0:
            pl.semaphore_wait(barrier, len(greeted))
            greet(met.at[0], [at(here, 1), at(here, -1)])
        send(xs.at[i], xr.at[i], core_s.at[i], core_r.at[i], sibling)
        yield
        mine = part(128 * core)
        landing(xr.at[i], core_s.at[i], core_r.at[i])
        both = mine + xr[i].astype(F32)
        hs[i] = both.astype(BF16)
        keep[i] = both
        for m in (5, 4, 7, 3, 6, 2, 1):
            send(
                hs.at[i, rows(16 * chip_of(m), 16)], rr.at[i, m - 1],
                sum_s.at[i, m - 1], sum_r.at[i, m - 1], in_row(m),
            )
        yield
        total = keep[i, rows(16 * chip, 16), :]
        for m in (1, 2, 6, 3, 7, 4, 5):
            landing(rr.at[i, m - 1], sum_s.at[i, m - 1], sum_r.at[i, m - 1])
            total = total + rr[i, m - 1].astype(F32)

        def piece(half, m):
            return full.at[turn, rows(256 * c + 128 * half + 16 * chip_of(m), 16)]

        own_piece = piece(core, 0)
        own_piece[...] = total.astype(BF16)
        for m in (5, 4, 7, 3, 6, 2, 1):
            send(own_piece, own_piece, all_s.at[i, m - 1], all_r.at[i, m - 1], in_row(m))
        send(own_piece, own_piece, relay_s.at[i, 0], relay_r.at[i, 0], sibling)
        yield
        for m in (1, 2, 6, 3, 7, 4, 5):
            landing(piece(core, m), all_s.at[i, m - 1], all_r.at[i, m - 1])
            send(piece(core, m), piece(core, m), relay_s.at[i, m], relay_r.at[i, m], sibling)
        for m in range(8):
            landing(piece(1 - core, m), relay_s.at[i, m], relay_r.at[i, m])

    def chunk(c):
        yield from row_sum(
            0, c, lambda r: dot(lt[pl.ds(pl.multiple_of(256 * c + r, 128), 128), :], g[...])
        )

        value = packed(dot(full[0, 256 * c : 256 * c + 256, :], q[...]))
        own[c] = value
        ps[c] = value.astype(BF16)
        if c == 0:
            pl.semaphore_wait(met.at[3], 1)
        for n, (plane, o) in enumerate(partners):
            send(
                ps.at[c, rows(64 * (plane * QUAD + moved(o) % QUAD), 64)], bq.at[c, n],
                near_s.at[c, n], near_r.at[c, n], at(plane, o),
            )
        yield
        total = own[c, rows(64 * (here * QUAD + z % QUAD), 64), :]
        for n in (4, 5, 6, 3, 1, 2, 0):
            landing(bq.at[c, n], near_s.at[c, n], near_r.at[c, n])
            total = total + bq[c, n].astype(F32)
        near[c] = total
        bs[c] = total.astype(BF16)
        if c == 0:
            pl.semaphore_wait(met.at[2], 2)
        for t in (2, 1, 3):
            send(
                bs.at[c, rows(16 * ((z // QUAD + t) % QUAD), 16)], br.at[c, t - 1],
                far_s.at[c, t - 1], far_r.at[c, t - 1], at(here, QUAD * t),
            )
        yield
        total = near[c, rows(16 * (z // QUAD), 16), :]
        for t in (1, 3, 2):
            landing(br.at[c, t - 1], far_s.at[c, t - 1], far_r.at[c, t - 1])
            total = total + br[c, t - 1].astype(F32)
        total = unpacked(total)
        mine = slice(8 * c, 8 * c + 8)
        projected_ref[mine, :] = total
        first = 0.9 * m1[mine, :] + 0.1 * total
        second = 0.95 * m2[mine, :] + 0.05 * total * total

        def slice_of(plane, o):
            zz = moved(o)
            return dirp.at[c, rows(16 * (plane * RING + (zz % QUAD) * QUAD + zz // QUAD), 16)]

        piece = slice_of(here, 0)
        piece[...] = packed(first / (jnp.sqrt(second) + 1e-08)).astype(BF16)
        for t in (2, 1, 3):
            send(piece, piece, dfar_s.at[c, t - 1], dfar_r.at[c, t - 1], at(here, QUAD * t))

        def forward(t):
            piece = slice_of(here, -QUAD * t)
            for n, (plane, o) in enumerate(partners):
                send(piece, piece, dnear_s.at[c, n, t], dnear_r.at[c, n, t], at(plane, o))

        forward(0)
        yield
        for t in (1, 3, 2):
            landing(slice_of(here, -QUAD * t), dfar_s.at[c, t - 1], dfar_r.at[c, t - 1])
            forward(t)
        yield
        for t in (0, 1, 3, 2):
            for n, (plane, o) in enumerate(partners):
                landing(slice_of(plane, -o - QUAD * t), dnear_s.at[c, n, t], dnear_r.at[c, n, t])
        dirf[c] = unpacked(dirp[c].astype(F32)).astype(BF16)
        yield from row_sum(1, c, lambda r: dot(dirf[c, rows(r, 128), :], qt[...]))
        done = pltpu.make_async_copy(
            full.at[1, pl.ds(256 * c, 256)], back_hbm.at[pl.ds(256 * c, 256)], out_sem.at[c]
        )
        done.start()
        finals.append(done)

    finals = []
    chunks = [chunk(0), chunk(1)]
    step = 0
    while chunks:
        for each in list(chunks):
            if next(each, finals) is finals:
                chunks.remove(each)
        step += 1
        if step == 2:
            loads[2].wait()
            qt[...] = q[...].T
            pl.semaphore_wait(met.at[0], 2)
            greet(met.at[1], [at(here, 2), at(here, -2)])
            greet(met.at[3], [at(there, 0)])
        if step == 3:
            lp[...] = lt[...].T
            left = pltpu.make_async_copy(lp, left_hbm, out_sem.at[2])
            left.start()
            finals.append(left)
            loads[3].wait()
            loads[4].wait()
            pl.semaphore_wait(met.at[1], 2)
            greet(met.at[2], [at(here, 4), at(here, -4)])
    for copy in sent:
        copy.wait_send()
    for copy in finals:
        copy.wait()


def finish(
    left_hbm, back_hbm, projected_hbm, m1_hbm, m2_hbm, update_hbm, first_hbm, second_hbm,
    left, back, projected, m1, m2, update, in_sem, out_sem,
):
    half = back.shape[0] // 2
    pairs = (
        (left_hbm, left),
        (back_hbm.at[pl.ds(0, half)], back.at[pl.ds(0, half)]),
        (back_hbm.at[pl.ds(half, half)], back.at[pl.ds(half, half)]),
        (projected_hbm, projected), (m1_hbm, m1), (m2_hbm, m2),
    )
    loads = [pltpu.make_async_copy(src, dst, in_sem.at[n]) for n, (src, dst) in enumerate(pairs)]
    for load in loads:
        load.start()
    for load in loads[3:]:
        load.wait()
    value = projected[...]
    m1[...] = 0.9 * m1[...] + 0.1 * value
    m2[...] = 0.95 * m2[...] + 0.05 * value * value
    stores = [
        pltpu.make_async_copy(m1, first_hbm, out_sem.at[0]),
        pltpu.make_async_copy(m2, second_hbm, out_sem.at[1]),
    ]
    for store in stores:
        store.start()
    for load in loads[:3]:
        load.wait()
    for n in range(4):
        block = pl.ds(128 * n, 128)
        update[block, :] = dot(left[block, :], back[...]).astype(BF16)
        store = pltpu.make_async_copy(update.at[block], update_hbm.at[block], out_sem.at[2 + n])
        store.start()
        stores.append(store)
    for store in stores:
        store.wait()


def per_device(gradient, left_basis, right_basis, first_moment, second_moment):
    depth, width = gradient.shape
    window = left_basis.shape[1]
    cols = right_basis.shape[1]
    mine = first_moment.shape[0]
    sems = pltpu.SemaphoreType.DMA
    back, left, projected = pl.pallas_call(
        kernel,
        out_shape=(
            jax.ShapeDtypeStruct((window, width), BF16),
            jax.ShapeDtypeStruct((depth, window), BF16),
            jax.ShapeDtypeStruct((mine, cols), F32),
        ),
        in_specs=[pl.BlockSpec(memory_space=pl.ANY)] * 5,
        out_specs=[pl.BlockSpec(memory_space=pl.ANY)] * 2 + [pl.BlockSpec(memory_space=pltpu.VMEM)],
        scratch_shapes=[
            pltpu.VMEM((depth, width), BF16),
            pltpu.VMEM((depth, window), BF16),
            pltpu.VMEM((width, cols), BF16),
            pltpu.VMEM((mine, cols), F32),
            pltpu.VMEM((mine, cols), F32),
            pltpu.VMEM((window, depth), BF16),
            pltpu.VMEM((depth, window), BF16),
            pltpu.VMEM((cols, width), BF16),
            pltpu.VMEM((4, 128, width), BF16),
            pltpu.VMEM((4, 128, width), BF16),
            pltpu.VMEM((4, 128, width), BF16),
            pltpu.VMEM((4, 7, 16, width), BF16),
            pltpu.VMEM((4, 128, width), F32),
            pltpu.VMEM((2, window, width), BF16),
            pltpu.VMEM((2, window, cols // 2), F32),
            pltpu.VMEM((2, window, cols // 2), BF16),
            pltpu.VMEM((2, 7, 64, cols // 2), BF16),
            pltpu.VMEM((2, 64, cols // 2), F32),
            pltpu.VMEM((2, 64, cols // 2), BF16),
            pltpu.VMEM((2, 3, mine, cols // 2), BF16),
            pltpu.VMEM((2, window, cols // 2), BF16),
            pltpu.VMEM((2, window // 2, cols), BF16),
            sems((5,)), sems((3,)),
            sems((4,)), sems((4,)),
            sems((4, 7)), sems((4, 7)),
            sems((4, 7)), sems((4, 7)),
            sems((4, 8)), sems((4, 8)),
            sems((2, 7)), sems((2, 7)),
            sems((2, 3)), sems((2, 3)),
            sems((2, 3)), sems((2, 3)),
            sems((2, 7, 4)), sems((2, 7, 4)),
            pltpu.SemaphoreType.REGULAR((4,)),
        ],
        compiler_params=pltpu.CompilerParams(
            collective_id=0, has_side_effects=True, vmem_limit_bytes=60 << 20
        ),
        name="soap",
    )(gradient, left_basis, right_basis, first_moment, second_moment)
    return pl.pallas_call(
        finish,
        out_shape=(
            jax.ShapeDtypeStruct((depth, width), BF16),
            jax.ShapeDtypeStruct(first_moment.shape, F32),
            jax.ShapeDtypeStruct(second_moment.shape, F32),
        ),
        in_specs=[pl.BlockSpec(memory_space=pl.ANY)] * 5,
        out_specs=[pl.BlockSpec(memory_space=pl.ANY)] * 3,
        scratch_shapes=[
            pltpu.VMEM((depth, window), BF16),
            pltpu.VMEM((window, width), BF16),
            pltpu.VMEM((mine, cols), F32),
            pltpu.VMEM((mine, cols), F32),
            pltpu.VMEM((mine, cols), F32),
            pltpu.VMEM((depth, width), BF16),
            sems((6,)), sems((6,)),
        ],
        compiler_params=pltpu.CompilerParams(vmem_limit_bytes=60 << 20),
        name="finish",
    )(left, back, projected, first_moment, second_moment)


def solution(mesh):
    placed = (
        P("row", "loop"),
        P("row", None),
        P("loop", "row"),
        P("loop", "row"),
        P("loop", "row"),
    )
    return jax.shard_map(
        per_device,
        mesh=mesh,
        in_specs=placed,
        out_specs=(P("row", "loop"), P("loop", "row"), P("loop", "row")),
        check_vma=False,
    )
```

```python
import functools

import jax
import jax.numpy as jnp
from jax import lax
from jax.experimental import pallas as pl
from jax.experimental.pallas import tpu as pltpu
from jax.sharding import PartitionSpec as P

MESH = pl.DeviceIdType.MESH
BF16 = jnp.bfloat16
F32 = jnp.float32
RING = 16
QUAD = 4


def dot(a, b):
    return jnp.dot(a, b, preferred_element_type=F32)


def kernel(
    g_hbm, l_hbm, q_hbm, m1_hbm, m2_hbm,
    back_hbm, left_hbm, projected_ref,
    g, lb, q, m1, m2, lt, lp, qt,
    xs, xr, hs, rr, keep, full,
    own, ps, bq, near, bs, br, dirp, dirf,
    in_sem, out_sem, core_s, core_r, sum_s, sum_r, all_s, all_r, relay_s, relay_r,
    near_s, near_r, far_s, far_r, dfar_s, dfar_r, dnear_s, dnear_r, met,
):
    row, loop = lax.axis_index("row"), lax.axis_index("loop")
    core, x, y = row % 2, (row // 2) % 2, row // 4
    here, z = loop // RING, loop % RING
    there = 1 - here
    chip = y * 2 + x
    offsets = (2 - 4 * core, 1, -1)
    partners = [(there, o) for o in offsets] + [(there, 0)] + [(here, o) for o in offsets]
    sibling = (row + 1 - 2 * core, loop)

    loads = [
        pltpu.make_async_copy(src, dst, in_sem.at[n])
        for n, (src, dst) in enumerate(
            ((l_hbm, lb), (g_hbm, g), (q_hbm, q), (m1_hbm, m1), (m2_hbm, m2))
        )
    ]
    for load in loads:
        load.start()

    def chip_of(m):
        py = y
        if m & 2:
            py = py + 1 - 2 * (py % 2)
        if m & 4:
            py = (py + 2) % 4
        px = 1 - x if m & 1 else x
        return py * 2 + px

    def in_row(m):
        return (chip_of(m) * 2 + core, loop)

    def moved(o):
        return (z + o + RING) % RING

    def at(plane, o):
        return (row, plane * RING + moved(o))

    barrier = pltpu.get_barrier_semaphore()
    greeted = [at(here, 1), at(here, -1), at(there, 0)] + [in_row(m) for m in range(1, 8)] + [sibling]

    def greet(sem, devices):
        for device in devices:
            pl.semaphore_signal(sem, inc=1, device_id=device, device_id_type=MESH)

    greet(barrier, greeted)

    loads[0].wait()
    lb[...] = lb[...].T
    for plane in range(2):
        for s in range(QUAD):
            for a in range(0, QUAD, 2):
                two = [
                    lb[16 * (plane * RING + i * QUAD + s) : 16 * (plane * RING + i * QUAD + s + 1), :].astype(F32)
                    for i in (a, a + 1)
                ]
                for c in range(2):
                    dst = 256 * c + 128 * plane + 32 * s + 8 * a
                    lt[dst : dst + 16, :] = jnp.concatenate(
                        [v[8 * c : 8 * c + 8] for v in two], axis=0
                    ).astype(BF16)
    loads[1].wait()

    sent = []

    def send(src, dst, s_sem, r_sem, device):
        copy = pltpu.make_async_remote_copy(
            src_ref=src, dst_ref=dst, send_sem=s_sem, recv_sem=r_sem,
            device_id=device, device_id_type=MESH,
        )
        copy.start()
        sent.append(copy)

    def landing(dst, s_sem, r_sem):
        pltpu.make_async_remote_copy(
            src_ref=dst, dst_ref=dst, send_sem=s_sem, recv_sem=r_sem,
            device_id=sibling, device_id_type=MESH,
        ).wait_recv()

    def rows(start, count):
        return pl.ds(pl.multiple_of(start, count), count)

    def packed(value):
        n, w = value.shape[0] // 8, value.shape[1] // 2
        value = value.reshape(n, 8, 2 * w)
        return jnp.concatenate([value[:, :, :w], value[:, :, w:]], axis=1).reshape(16 * n, w)

    def unpacked(value):
        n, w = value.shape[0] // 16, value.shape[1]
        value = value.reshape(n, 16, w)
        return jnp.concatenate([value[:, :8], value[:, 8:]], axis=2).reshape(8 * n, 2 * w)

    def row_sum(turn, c, part):
        i = 2 * turn + c
        xs[i] = part(128 * (1 - core)).astype(BF16)
        if i == 0:
            pl.semaphore_wait(barrier, len(greeted))
            greet(met.at[0], [at(here, 1), at(here, -1)])
        send(xs.at[i], xr.at[i], core_s.at[i], core_r.at[i], sibling)
        yield
        mine = part(128 * core)
        landing(xr.at[i], core_s.at[i], core_r.at[i])
        both = mine + xr[i].astype(F32)
        hs[i] = both.astype(BF16)
        keep[i] = both
        for m in (3, 5, 7, 4, 2, 6, 1):
            send(
                hs.at[i, rows(16 * chip_of(m), 16)], rr.at[i, m - 1],
                sum_s.at[i, m - 1], sum_r.at[i, m - 1], in_row(m),
            )
        yield
        total = keep[i, rows(16 * chip, 16), :]
        for m in (1, 2, 6, 3, 7, 4, 5):
            landing(rr.at[i, m - 1], sum_s.at[i, m - 1], sum_r.at[i, m - 1])
            total = total + rr[i, m - 1].astype(F32)

        def piece(half, m):
            return full.at[turn, rows(256 * c + 128 * half + 16 * chip_of(m), 16)]

        own_piece = piece(core, 0)
        own_piece[...] = total.astype(BF16)
        for m in (3, 5, 7, 4, 2, 6, 1):
            send(own_piece, own_piece, all_s.at[i, m - 1], all_r.at[i, m - 1], in_row(m))
        send(own_piece, own_piece, relay_s.at[i, 0], relay_r.at[i, 0], sibling)
        yield
        for m in (1, 2, 6, 3, 7, 4, 5):
            landing(piece(core, m), all_s.at[i, m - 1], all_r.at[i, m - 1])
            send(piece(core, m), piece(core, m), relay_s.at[i, m], relay_r.at[i, m], sibling)
        for m in range(8):
            landing(piece(1 - core, m), relay_s.at[i, m], relay_r.at[i, m])

    def chunk(c):
        yield from row_sum(
            0, c, lambda r: dot(lt[pl.ds(pl.multiple_of(256 * c + r, 128), 128), :], g[...])
        )

        value = packed(dot(full[0, 256 * c : 256 * c + 256, :], q[...]))
        own[c] = value
        ps[c] = value.astype(BF16)
        if c == 0:
            pl.semaphore_wait(met.at[3], 1)
        for n, (plane, o) in enumerate(partners):
            send(
                ps.at[c, rows(64 * (plane * QUAD + moved(o) % QUAD), 64)], bq.at[c, n],
                near_s.at[c, n], near_r.at[c, n], at(plane, o),
            )
        yield
        total = own[c, rows(64 * (here * QUAD + z % QUAD), 64), :]
        for n in (4, 5, 6, 3, 1, 2, 0):
            landing(bq.at[c, n], near_s.at[c, n], near_r.at[c, n])
            total = total + bq[c, n].astype(F32)
        near[c] = total
        bs[c] = total.astype(BF16)
        if c == 0:
            pl.semaphore_wait(met.at[2], 2)
        for t in (2, 1, 3):
            send(
                bs.at[c, rows(16 * ((z // QUAD + t) % QUAD), 16)], br.at[c, t - 1],
                far_s.at[c, t - 1], far_r.at[c, t - 1], at(here, QUAD * t),
            )
        yield
        total = near[c, rows(16 * (z // QUAD), 16), :]
        for t in (1, 3, 2):
            landing(br.at[c, t - 1], far_s.at[c, t - 1], far_r.at[c, t - 1])
            total = total + br[c, t - 1].astype(F32)
        total = unpacked(total)
        mine = slice(8 * c, 8 * c + 8)
        projected_ref[mine, :] = total
        first = 0.9 * m1[mine, :] + 0.1 * total
        second = 0.95 * m2[mine, :] + 0.05 * total * total

        def slice_of(plane, o):
            zz = moved(o)
            return dirp.at[c, rows(16 * (plane * RING + (zz % QUAD) * QUAD + zz // QUAD), 16)]

        piece = slice_of(here, 0)
        piece[...] = packed(first / (jnp.sqrt(second) + 1e-08)).astype(BF16)
        for t in (2, 1, 3):
            send(piece, piece, dfar_s.at[c, t - 1], dfar_r.at[c, t - 1], at(here, QUAD * t))

        def forward(t):
            piece = slice_of(here, -QUAD * t)
            for n, (plane, o) in enumerate(partners):
                send(piece, piece, dnear_s.at[c, n, t], dnear_r.at[c, n, t], at(plane, o))

        forward(0)
        yield
        for t in (1, 3, 2):
            landing(slice_of(here, -QUAD * t), dfar_s.at[c, t - 1], dfar_r.at[c, t - 1])
            forward(t)
        yield
        for t in (0, 1, 3, 2):
            for n, (plane, o) in enumerate(partners):
                landing(slice_of(plane, -o - QUAD * t), dnear_s.at[c, n, t], dnear_r.at[c, n, t])
        dirf[c] = unpacked(dirp[c].astype(F32)).astype(BF16)
        yield from row_sum(1, c, lambda r: dot(dirf[c, rows(r, 128), :], qt[...]))
        done = pltpu.make_async_copy(
            full.at[1, pl.ds(256 * c, 256)], back_hbm.at[pl.ds(256 * c, 256)], out_sem.at[c]
        )
        done.start()
        finals.append(done)

    finals = []
    marks = []
    settled = [0]

    def settle(count):
        for copy in sent[settled[0] : count]:
            copy.wait_send()
        settled[0] = count

    chunks = [chunk(0), chunk(1)]
    step = 0
    while chunks:
        for each in list(chunks):
            if next(each, finals) is finals:
                chunks.remove(each)
        step += 1
        marks.append(len(sent))
        if step > 2:
            settle(marks[step - 3])
        if step == 2:
            loads[2].wait()
            qt[...] = q[...].T
            pl.semaphore_wait(met.at[0], 2)
            greet(met.at[1], [at(here, 2), at(here, -2)])
            greet(met.at[3], [at(there, 0)])
        if step == 3:
            lp[...] = lt[...].T
            left = pltpu.make_async_copy(lp, left_hbm, out_sem.at[2])
            left.start()
            finals.append(left)
            loads[3].wait()
            loads[4].wait()
            pl.semaphore_wait(met.at[1], 2)
            greet(met.at[2], [at(here, 4), at(here, -4)])
    settle(len(sent))
    for copy in finals:
        copy.wait()


def finish(
    left_hbm, back_hbm, projected_hbm, m1_hbm, m2_hbm, update_hbm, first_hbm, second_hbm,
    left, back, projected, m1, m2, update, in_sem, out_sem,
):
    half = back.shape[0] // 2
    pairs = (
        (left_hbm, left),
        (back_hbm.at[pl.ds(0, half)], back.at[pl.ds(0, half)]),
        (back_hbm.at[pl.ds(half, half)], back.at[pl.ds(half, half)]),
        (projected_hbm, projected), (m1_hbm, m1), (m2_hbm, m2),
    )
    loads = [pltpu.make_async_copy(src, dst, in_sem.at[n]) for n, (src, dst) in enumerate(pairs)]
    for load in loads:
        load.start()
    for load in loads[3:]:
        load.wait()
    value = projected[...]
    m1[...] = 0.9 * m1[...] + 0.1 * value
    m2[...] = 0.95 * m2[...] + 0.05 * value * value
    stores = [
        pltpu.make_async_copy(m1, first_hbm, out_sem.at[0]),
        pltpu.make_async_copy(m2, second_hbm, out_sem.at[1]),
    ]
    for store in stores:
        store.start()
    for load in loads[:3]:
        load.wait()
    for n in range(4):
        block = pl.ds(128 * n, 128)
        update[block, :] = dot(left[block, :], back[...]).astype(BF16)
        store = pltpu.make_async_copy(update.at[block], update_hbm.at[block], out_sem.at[2 + n])
        store.start()
        stores.append(store)
    for store in stores:
        store.wait()


def per_device(gradient, left_basis, right_basis, first_moment, second_moment):
    depth, width = gradient.shape
    window = left_basis.shape[1]
    cols = right_basis.shape[1]
    mine = first_moment.shape[0]
    sems = pltpu.SemaphoreType.DMA
    back, left, projected = pl.pallas_call(
        kernel,
        out_shape=(
            jax.ShapeDtypeStruct((window, width), BF16),
            jax.ShapeDtypeStruct((depth, window), BF16),
            jax.ShapeDtypeStruct((mine, cols), F32),
        ),
        in_specs=[pl.BlockSpec(memory_space=pl.ANY)] * 5,
        out_specs=[pl.BlockSpec(memory_space=pl.ANY)] * 2 + [pl.BlockSpec(memory_space=pltpu.VMEM)],
        scratch_shapes=[
            pltpu.VMEM((depth, width), BF16),
            pltpu.VMEM((depth, window), BF16),
            pltpu.VMEM((width, cols), BF16),
            pltpu.VMEM((mine, cols), F32),
            pltpu.VMEM((mine, cols), F32),
            pltpu.VMEM((window, depth), BF16),
            pltpu.VMEM((depth, window), BF16),
            pltpu.VMEM((cols, width), BF16),
            pltpu.VMEM((4, 128, width), BF16),
            pltpu.VMEM((4, 128, width), BF16),
            pltpu.VMEM((4, 128, width), BF16),
            pltpu.VMEM((4, 7, 16, width), BF16),
            pltpu.VMEM((4, 128, width), F32),
            pltpu.VMEM((2, window, width), BF16),
            pltpu.VMEM((2, window, cols // 2), F32),
            pltpu.VMEM((2, window, cols // 2), BF16),
            pltpu.VMEM((2, 7, 64, cols // 2), BF16),
            pltpu.VMEM((2, 64, cols // 2), F32),
            pltpu.VMEM((2, 64, cols // 2), BF16),
            pltpu.VMEM((2, 3, mine, cols // 2), BF16),
            pltpu.VMEM((2, window, cols // 2), BF16),
            pltpu.VMEM((2, window // 2, cols), BF16),
            sems((5,)), sems((3,)),
            sems((4,)), sems((4,)),
            sems((4, 7)), sems((4, 7)),
            sems((4, 7)), sems((4, 7)),
            sems((4, 8)), sems((4, 8)),
            sems((2, 7)), sems((2, 7)),
            sems((2, 3)), sems((2, 3)),
            sems((2, 3)), sems((2, 3)),
            sems((2, 7, 4)), sems((2, 7, 4)),
            pltpu.SemaphoreType.REGULAR((4,)),
        ],
        compiler_params=pltpu.CompilerParams(
            collective_id=0, has_side_effects=True, vmem_limit_bytes=60 << 20
        ),
        name="soap",
    )(gradient, left_basis, right_basis, first_moment, second_moment)
    return pl.pallas_call(
        finish,
        out_shape=(
            jax.ShapeDtypeStruct((depth, width), BF16),
            jax.ShapeDtypeStruct(first_moment.shape, F32),
            jax.ShapeDtypeStruct(second_moment.shape, F32),
        ),
        in_specs=[pl.BlockSpec(memory_space=pl.ANY)] * 5,
        out_specs=[pl.BlockSpec(memory_space=pl.ANY)] * 3,
        scratch_shapes=[
            pltpu.VMEM((depth, window), BF16),
            pltpu.VMEM((window, width), BF16),
            pltpu.VMEM((mine, cols), F32),
            pltpu.VMEM((mine, cols), F32),
            pltpu.VMEM((mine, cols), F32),
            pltpu.VMEM((depth, width), BF16),
            sems((6,)), sems((6,)),
        ],
        compiler_params=pltpu.CompilerParams(vmem_limit_bytes=60 << 20),
        name="finish",
    )(left, back, projected, first_moment, second_moment)


def solution(mesh):
    placed = (
        P("row", "loop"),
        P("row", None),
        P("loop", "row"),
        P("loop", "row"),
        P("loop", "row"),
    )
    return jax.shard_map(
        per_device,
        mesh=mesh,
        in_specs=placed,
        out_specs=(P("row", "loop"), P("loop", "row"), P("loop", "row")),
        check_vma=False,
    )
```
